32 devices in a mesh: blk: 8 (over z, y), span: 4 (over x, core).
Axes of the slice: x: 2, y: 2, z: 4, core: 2. Of those that a mesh axis runs over, the one named last changes fastest.
Arguments:
- stiffness: float32 [128, 128], P('span'), may hold values from -1 to 8, as said below
- mistune_table: float32 [8, 128], P(None, 'span'), may hold values from 0.2 to 2
- sector_class: int32 [8], P('blk'), may hold values from 0 to 7
- lumped_mass: float32 [8, 128], P('blk', 'span'), may hold values from 0.5 to 2
- near_faces: int32 [8, 32], P('blk'), may hold values from 0 to 127
- far_faces: int32 [8, 32], P('blk'), may hold values from 0 to 127
- contact_state: int32 [8, 32], P('blk'), may hold values 0 or 1
- displacement: float32 [8, 128, 128], P('blk', 'span'), may hold values from -6 to 6
- velocity: float32 [8, 128, 128], P('blk', 'span'), may hold values from -6 to 6
- acceleration: float32 [8, 128, 128], P('blk', 'span'), may hold values from -6 to 6
- load_steps: float32 [2, 8, 128, 128], P(None, 'blk', 'span'), may hold values from -6 to 6
Outputs:
- new_displacement: float32 [8, 128, 128], P('blk', 'span')
- new_velocity: float32 [8, 128, 128], P('blk', 'span')
- new_acceleration: float32 [8, 128, 128], P('blk', 'span')
The draws below stay inside these ranges and needn't reach their ends.
Inputs may be any that keep to these rules, and one draw needn't show every extreme that they name: stiffness is symmetric.
All inputs are finite; a program needn't handle non-finite values. No bound on the sum of `contact_state` on one device may be relied on, other than what follows from the above.
Results may differ from the reference program's by a relative error of at most 0.0003.
Values sent between devices are 32-bit elements; how exact they have to be, the bound alone decides.
A program may use at most 64 MiB of HBM per device.

```python
import math
import jax
import jax.numpy as jnp
from jax import lax

NRHS = 128
BND = 64
FACE = 32
CLASSES = 8
STEPS = 2
ITERS = 5
SECTORS = 8
DOF_SEC = 128


def draw_stiffness(key, part):
    key = jax.random.fold_in(key, 11)
    first_key, second_key = jax.random.split(key)
    rough = jnp.clip(jax.random.normal(first_key, (DOF_SEC, DOF_SEC), jnp.float32), -4.0, 4.0)
    symmetric = (rough + rough.T) / jnp.sqrt(2.0 * DOF_SEC)
    diagonal = jax.random.uniform(second_key, (DOF_SEC,), jnp.float32, 4.0, 8.0)
    identity = jnp.eye(DOF_SEC, dtype=jnp.float32)
    return symmetric * (1.0 - identity) + identity * diagonal[:, None]


def set_ends(entries, stream_key, low, largest):
    index_at = [jax.random.randint(jax.random.fold_in(stream_key, axis), (), 0, length) for axis, length in enumerate(entries.shape)]
    widest = entries.shape.index(max(entries.shape))
    next_to = index_at[:widest] + [(index_at[widest] + 1) % entries.shape[widest]] + index_at[widest + 1:]
    return entries.at[tuple(index_at)].set(low).at[tuple(next_to)].set(largest)


def steps_of(key, dims, pieces, least, largest):
    def one(dim, parts):
        steps = jax.random.uniform(jax.random.fold_in(jax.random.fold_in(key, 6), dim), (parts,), jnp.float32, least / len(pieces), largest / len(pieces))
        return jnp.repeat(jnp.exp(steps), dims[dim] // parts).reshape((-1,) + (1,) * (len(dims) - dim - 1))

    gain = one(*pieces[0])
    for cut in pieces[1:]:
        gain = gain * one(*cut)
    return gain


def centred(stream_key, dims, width, most, shards=(), kind=jnp.bfloat16):
    gain = steps_of(stream_key, dims, shards, -0.22, 0.18) if shards else 1.0
    drawn = jax.random.normal(stream_key, dims, jnp.float32) * width * gain
    return jnp.minimum(jnp.maximum(drawn, -most), most).astype(kind)


def setup_inputs(seed: int = 0) -> dict:
    key_list = jax.random.split(jax.random.key(seed), 12)
    return {
        "stiffness": draw_stiffness(jax.random.fold_in(key_list[11], 71), 0),
        "mistune_table": jnp.clip(jnp.exp(math.log(2.0) - 2.3025851 * jax.random.uniform(key_list[1], (CLASSES, DOF_SEC), jnp.float32) ** steps_of(key_list[1], (CLASSES, DOF_SEC), ((1, 4),), -0.2, 0.2)), 0.2, 2.0),
        "sector_class": set_ends(jax.random.randint(key_list[2], (SECTORS,), 0, CLASSES), jax.random.fold_in(key_list[2], 1), 0, CLASSES - 1).astype(jnp.int32),
        "lumped_mass": jnp.clip(jnp.exp(math.log(2.0) - 1.3862944 * jax.random.uniform(key_list[3], (SECTORS, DOF_SEC), jnp.float32) ** steps_of(key_list[3], (SECTORS, DOF_SEC), ((0, 8), (1, 4)), -0.2, 0.2)), 0.5, 2.0),
        "near_faces": set_ends(jax.random.randint(key_list[4], (SECTORS, FACE), 0, DOF_SEC), jax.random.fold_in(key_list[4], 1), 0, DOF_SEC - 1).astype(jnp.int32),
        "far_faces": set_ends(jax.random.randint(key_list[5], (SECTORS, FACE), 0, DOF_SEC), jax.random.fold_in(key_list[5], 1), 0, DOF_SEC - 1).astype(jnp.int32),
        "contact_state": set_ends((jax.random.randint(key_list[6], (SECTORS, FACE), 0, 2) < 1).astype(jnp.int32), jax.random.fold_in(key_list[6], 1), 0, 1),
        "displacement": centred(key_list[7], (SECTORS, DOF_SEC, NRHS), 1.0, 6.0, ((0, 8), (1, 4)), jnp.float32),
        "velocity": centred(key_list[8], (SECTORS, DOF_SEC, NRHS), 1.0, 6.0, ((0, 8), (1, 4)), jnp.float32),
        "acceleration": centred(key_list[9], (SECTORS, DOF_SEC, NRHS), 1.0, 6.0, ((0, 8), (1, 4)), jnp.float32),
        "load_steps": centred(key_list[10], (STEPS, SECTORS, DOF_SEC, NRHS), 1.0, 6.0, ((1, 8), (2, 4)), jnp.float32),
    }


highest = lax.Precision.HIGHEST
stick_rate = 20.0
slip_rate = 0.5
cycle_rate = 4.0


def stiff_apply(vector, stiffness, extra_diag, contact_rates, near_faces, far_faces):
    sector_width = vector.shape[1]
    product = jnp.einsum("rk,skc->src", stiffness, vector, precision=highest)
    total_force = product + extra_diag[:, :, None] * vector
    left_rows = vector[:, :BND]
    right_rows = vector[:, sector_width - BND:]
    total_force = total_force.at[:, :BND].add(cycle_rate * (left_rows - jnp.roll(right_rows, 1, 0)))
    total_force = total_force.at[:, sector_width - BND:].add(cycle_rate * (right_rows - jnp.roll(left_rows, -1, 0)))
    after_sector = jnp.roll(vector, -1, 0)
    take_rows = jax.vmap(lambda values, indices: values[indices])
    damper_force = contact_rates[:, :, None] * (take_rows(vector, near_faces) - take_rows(after_sector, far_faces))
    add_rows = jax.vmap(lambda target, indices, amounts: target.at[indices].add(amounts))
    total_force = add_rows(total_force, near_faces, damper_force)
    total_force = total_force + jnp.roll(add_rows(jnp.zeros_like(vector), far_faces, -damper_force), 1, 0)
    return total_force


def reference(stiffness, mistune_table, sector_class, lumped_mass, near_faces, far_faces, contact_state, displacement, velocity, acceleration, load_steps):
    extra_diag = mistune_table[sector_class]
    contact_rates = jnp.where(contact_state == 1, stick_rate, slip_rate).astype(jnp.float32)
    mass_cols = lumped_mass[:, :, None]

    def stiff_op(vector):
        return stiff_apply(vector, stiffness, extra_diag, contact_rates, near_faces, far_faces)

    for newmark_step in range(STEPS):
        predicted = displacement + velocity + 0.25 * acceleration
        residual = load_steps[newmark_step] - mass_cols * acceleration - stiff_op(predicted + 0.25 * acceleration)
        solution = acceleration
        direction = residual
        norm_now = jnp.sum(residual * residual, axis=(0, 1))
        for iteration in range(ITERS):
            image = mass_cols * direction + 0.25 * stiff_op(direction)
            step_length = norm_now / jnp.sum(direction * image, axis=(0, 1))
            solution = solution + step_length * direction
            residual = residual - step_length * image
            norm_next = jnp.sum(residual * residual, axis=(0, 1))
            direction = residual + (norm_next / norm_now) * direction
            norm_now = norm_next
        displacement = predicted + 0.25 * solution
        velocity = velocity + 0.5 * (acceleration + solution)
        acceleration = solution
    return displacement, velocity, acceleration
```

```python
import functools

import jax
import jax.numpy as jnp
from jax import lax
from jax.experimental import pallas as pl
from jax.experimental.pallas import tpu as pltpu
from jax.sharding import PartitionSpec as P

BND = 64
STEPS = 2
ITERS = 5


highest = lax.Precision.HIGHEST
stick_rate = 20.0
slip_rate = 0.5
cycle_rate = 4.0

MESH = pl.DeviceIdType.MESH
LANES = 128
SUB = 8
CASES = 4
f32, bf16 = jnp.float32, jnp.bfloat16


def passed_along(block, axis, distance):
    devices = range(lax.axis_size(axis))
    route = [((i - distance) % len(devices), i) for i in devices]
    return lax.ppermute(block, axis, route)


def column_norm(vector):
    return lax.psum(jnp.sum(vector * vector, axis=(0, 1)), ("blk", "span"))


def shards(
    stiffness,
    mistune_table,
    sector_class,
    lumped_mass,
    near_faces,
    far_faces,
    contact_state,
    displacement,
    velocity,
    acceleration,
    load_steps,
):
    sectors_here, rows_here, columns = displacement.shape
    sector_width = stiffness.shape[1]
    offset = lax.axis_index("span") * rows_here
    prior_face, prior_state = passed_along((far_faces[-1], contact_state[-1]), "blk", 1)
    contact_rates = jnp.where(contact_state == 1, stick_rate, slip_rate).astype(jnp.float32)
    prior_rate = jnp.where(prior_state == 1, stick_rate, slip_rate).astype(jnp.float32)
    rate_in = jnp.concatenate([prior_rate[None], contact_rates[:-1]], 0)
    face_in = jnp.concatenate([prior_face[None], far_faces[:-1]], 0)
    left_index = jnp.arange(BND, dtype=jnp.int32)[None]
    right_index = left_index + (sector_width - BND)
    index_list = jnp.concatenate([left_index, right_index, near_faces, face_in], 1)
    face_count = near_faces.shape[1]
    row_ids = jnp.arange(rows_here, dtype=jnp.int32)
    placement_map = (index_list[:, :, None] - offset == row_ids[None, None, :]).astype(jnp.float32)
    class_ids = jnp.arange(mistune_table.shape[0], dtype=jnp.int32)
    class_map = (sector_class[:, None] == class_ids[None, :]).astype(jnp.float32)
    extra_diag = jnp.dot(class_map, mistune_table, precision=highest)
    mass_cols = lumped_mass[:, :, None]
    pick_rows = jax.vmap(lambda values, rows: values[rows])

    def stiff_op(vector):
        gathered = lax.all_gather(vector, "span", axis=1, tiled=True)
        product = jnp.einsum("rk,skc->src", stiffness, gathered, precision=highest)
        picked = pick_rows(gathered, index_list)
        left_values = picked[:, :BND]
        right_values = picked[:, BND : 2 * BND]
        near_values = picked[:, 2 * BND : 2 * BND + face_count]
        far_values = picked[:, 2 * BND + face_count :]
        prior_right, prior_near = passed_along((right_values[-1], near_values[-1]), "blk", 1)
        next_left, next_far = passed_along((left_values[0], far_values[0]), "blk", -1)
        after_left = jnp.concatenate([left_values[1:], next_left[None]], 0)
        before_right = jnp.concatenate([prior_right[None], right_values[:-1]], 0)
        after_far = jnp.concatenate([far_values[1:], next_far[None]], 0)
        before_near = jnp.concatenate([prior_near[None], near_values[:-1]], 0)
        force_left = cycle_rate * (left_values - before_right)
        force_right = cycle_rate * (right_values - after_left)
        force_out = contact_rates[:, :, None] * (near_values - after_far)
        force_in = -rate_in[:, :, None] * (before_near - far_values)
        weights = jnp.concatenate([force_left, force_right, force_out, force_in], 1)
        spread = jnp.einsum("sir,sic->src", placement_map, weights, precision=highest)
        return product + extra_diag[:, :, None] * vector + spread

    for newmark_step in range(STEPS):
        predicted = displacement + velocity + 0.25 * acceleration
        residual = (
            load_steps[newmark_step]
            - mass_cols * acceleration
            - stiff_op(predicted + 0.25 * acceleration)
        )
        solution = acceleration
        direction = residual
        norm_now = column_norm(residual)
        for iteration in range(ITERS):
            image = mass_cols * direction + 0.25 * stiff_op(direction)
            curve = lax.psum(jnp.sum(direction * image, axis=(0, 1)), ("blk", "span"))
            step_length = norm_now / curve
            solution = solution + step_length * direction
            residual = residual - step_length * image
            norm_next = column_norm(residual)
            direction = residual + norm_next / norm_now * direction
            norm_now = norm_next
        displacement = predicted + 0.25 * solution
        velocity = velocity + 0.5 * (acceleration + solution)
        acceleration = solution
    return (displacement, velocity, acceleration)


def lanes_dot(a, b):
    return lax.dot_general(a, b, (((1,), (1,)), ((), ())), preferred_element_type=f32)


def two_parts(x):
    high = x.astype(bf16).astype(f32)
    return high, x - high


def swap_halves(tile):
    return pltpu.roll(tile, CASES, 0)


def wheel_kernel(
    blks,
    spans,
    cls_ref,
    kst_ref,
    tab_ref,
    mass_ref,
    near_ref,
    far_ref,
    state_ref,
    disp_ref,
    vel_ref,
    acc_ref,
    load_ref,
    disp_out,
    vel_out,
    acc_out,
    send,
    recv,
    kfull,
    back_send,
    back_recv,
    onehot_near,
    onehot_far,
    weights,
    kweights,
    mass_s,
    diag_s,
    turned,
    send_sem,
    recv_sem,
    ksend_sem,
    krecv_sem,
    bsend_sem,
    brecv_sem,
):
    count = blks * spans
    blk, span = lax.axis_index("blk"), lax.axis_index("span")
    me = blk * spans + span
    rows = kst_ref.shape[0]
    width = kst_ref.shape[1]

    def other(k):
        there = lax.rem(me + k, count)
        return there, (there // spans, lax.rem(there, spans))

    barrier = pltpu.get_barrier_semaphore()
    for k in range(1, count):
        pl.semaphore_signal(barrier, inc=1, device_id=other(k)[1], device_id_type=MESH)

    row = lax.broadcasted_iota(jnp.int32, (SUB, LANES), 0)
    lane = lax.broadcasted_iota(jnp.int32, (SUB, LANES), 1)
    mine = (lane // rows) == span
    low = row < CASES

    class_row = lax.broadcasted_iota(jnp.int32, tab_ref.shape, 0)
    extra = jnp.sum(jnp.where(class_row == cls_ref[0], tab_ref[...], 0.0), axis=0, keepdims=True)
    mass_here = mass_ref[...]
    rate = jnp.where(state_ref[...] == 1, 0.25 * stick_rate, 0.25 * slip_rate).astype(f32)
    contact = jnp.concatenate([near_ref[...].astype(f32), far_ref[...].astype(f32), rate, rate], 1)
    wide_mass = jnp.where(mine, jnp.concatenate([mass_here] * spans, 1), 0.0)
    wide_extra = jnp.where(mine, jnp.concatenate([0.25 * extra] * spans, 1), 0.0)
    constants = jnp.where(
        row == CASES, wide_mass, jnp.where(row == CASES + 1, wide_extra, jnp.broadcast_to(contact, (SUB, LANES)))
    )

    disp, vel, acc = disp_ref[0], vel_ref[0], acc_ref[0]
    mass_col = jnp.sum(
        jnp.where(
            lax.broadcasted_iota(jnp.int32, (rows, rows), 0) == lax.broadcasted_iota(jnp.int32, (rows, rows), 1),
            jnp.broadcast_to(mass_here, (rows, rows)),
            0.0,
        ),
        axis=1,
        keepdims=True,
    )
    inertia = mass_col * acc
    ahead = disp + vel + 0.5 * acc
    later = ahead + vel + 1.5 * acc
    stacked = jnp.concatenate([ahead, load_ref[0, 0] - inertia, later, load_ref[1, 0] - inertia], 0)
    flipped = stacked.T
    for j in range(count // 2):
        tile = flipped[SUB * j : SUB * (j + 1)]
        send[2 * j] = jnp.where(low, tile, constants)
        send[2 * j + 1] = jnp.where(low, swap_halves(tile), constants)

    pl.semaphore_wait(barrier, count - 1)
    for k in range(1, spans):
        pltpu.make_async_remote_copy(
            src_ref=kst_ref,
            dst_ref=kfull.at[pl.ds(pl.multiple_of(span * rows, rows), rows)],
            send_sem=ksend_sem,
            recv_sem=krecv_sem,
            device_id=(blk, lax.rem(span + k, spans)),
            device_id_type=MESH,
        ).start()
    for k in range(1, count):
        there, place = other(k)
        pltpu.make_async_remote_copy(
            src_ref=send.at[there],
            dst_ref=recv.at[me],
            send_sem=send_sem,
            recv_sem=recv_sem,
            device_id=place,
            device_id_type=MESH,
        ).start()
    recv[me] = send[me]
    kfull[pl.ds(pl.multiple_of(span * rows, rows), rows), :] = kst_ref[...]

    rest = pl.ds(0, (spans - 1) * rows)
    pltpu.make_async_copy(kfull.at[rest], kfull.at[rest], krecv_sem).wait()
    kscaled = 0.25 * kfull[...]
    khigh, klow = two_parts(kscaled)
    kweights[:, :width] = khigh.astype(bf16)
    kweights[:, width:] = klow.astype(bf16)

    others = pl.ds(0, count - 1)
    pltpu.make_async_copy(recv.at[others], recv.at[others], recv_sem).wait()

    sub_index = lax.broadcasted_iota(jnp.int32, (width, LANES), 0).astype(f32)
    face_lane = lax.broadcasted_iota(jnp.int32, (1, LANES), 1) < near_ref.shape[1]
    ones = jnp.ones((2 * SUB, LANES), bf16)
    near_diag, far_diag, own = [], [], []
    for b in range(blks):
        tiles = [recv[b * spans + s] for s in range(spans)]
        total = tiles[0]
        for tile in tiles[1:]:
            total = total + tile
        own.append((total[CASES : CASES + 1], total[CASES + 1 : CASES + 2]))
        faces = tiles[0][CASES + 2 : CASES + 3]
        near_row = faces
        far_row = pltpu.roll(faces, LANES - near_ref.shape[1], 1)
        rate_row = jnp.where(face_lane, pltpu.roll(faces, LANES - 2 * near_ref.shape[1], 1), 0.0)
        near_hot = jnp.where(sub_index == near_row, rate_row, 0.0).astype(bf16)
        far_hot = jnp.where((sub_index == far_row) & face_lane, 1.0, 0.0).astype(bf16)
        onehot_near[b] = near_hot
        onehot_far[b] = far_hot
        near_diag.append(lanes_dot(ones, near_hot))
        far_diag.append(lanes_dot(jnp.broadcast_to(rate_row, (2 * SUB, LANES)).astype(bf16), far_hot))

    n_row = lax.broadcasted_iota(jnp.int32, (width, width), 0)
    n_col = lax.broadcasted_iota(jnp.int32, (width, width), 1)
    tie = 0.25 * cycle_rate
    shift_down = jnp.where((n_row == n_col + (width - BND)) & (n_col < BND), tie, 0.0)
    shift_up = jnp.where((n_col == n_row + (width - BND)) & (n_row < BND), tie, 0.0)
    lane_row = lax.broadcasted_iota(jnp.int32, (1, LANES), 1)
    ends = jnp.where(lane_row < BND, tie, 0.0) + jnp.where(lane_row >= width - BND, tie, 0.0)
    for b in range(blks):
        prev = (b - 1) % blks
        j, half = divmod(b, 2)
        mass_s[j, CASES * half : CASES * (half + 1), :] = jnp.broadcast_to(own[b][0], (CASES, LANES))
        diag_row = own[b][1] + ends + near_diag[b][0:1] + far_diag[prev][0:1]
        diag_s[j, CASES * half : CASES * (half + 1), :] = jnp.broadcast_to(diag_row, (CASES, LANES))
        before = -(lanes_dot(onehot_near[prev], onehot_far[prev]) + shift_down)
        after = -(lanes_dot(onehot_far[b], onehot_near[b]) + shift_up)
        group = j if half == 0 else (j + 1) % (blks // 2)
        base = 2 * width * half
        for part, block in enumerate((before, after)):
            high, small = two_parts(block)
            weights[group, width * part : width * (part + 1), base : base + width] = high.astype(bf16)
            weights[group, width * part : width * (part + 1), base + width : base + 2 * width] = small.astype(bf16)

    pairs = blks // 2
    group_of = lane // rows
    pieces = [[] for _ in range(4)]
    for j in range(pairs):
        parts = [
            jnp.where(low, recv[2 * j * spans + s], swap_halves(recv[(2 * j + 1) * spans + s])) for s in range(spans)
        ]
        for k in range(4):
            value = None
            for s in range(spans):
                turn = (rows * (s - k)) % LANES
                moved = pltpu.roll(parts[s], turn, 1) if turn else parts[s]
                value = moved if value is None else jnp.where(group_of == s, moved, value)
            pieces[k].append(value)
    u0, force0, u1, force1 = (jnp.stack(p) for p in pieces)
    mass = mass_s[...]
    diag = diag_s[...]

    def quarter_k(v):
        high, small = two_parts(v)
        both = jnp.concatenate([high.reshape(pairs * SUB, LANES), small.reshape(pairs * SUB, LANES)], 0).astype(bf16)
        p = jnp.dot(both, kweights[...], preferred_element_type=f32)
        h = pairs * SUB
        common = p[:h, :width] + (p[h:, :width] + p[:h, width:])
        tiles = []
        for j in range(pairs):
            t = jnp.concatenate([swap_halves(high[j]), swap_halves(small[j])], 0)
            tiles.append(t.astype(bf16))
        across = []
        for j in range(pairs):
            lhs = jnp.concatenate([tiles[j - 1], tiles[j]], 1)
            g = jnp.dot(lhs, weights[j], preferred_element_type=f32)
            even = g[:SUB, :width] + (g[SUB:, :width] + g[:SUB, width : 2 * width])
            odd = g[:SUB, 2 * width : 3 * width] + (g[SUB:, 2 * width : 3 * width] + g[:SUB, 3 * width :])
            across.append((even, odd))
        sides = jnp.stack([jnp.where(low, across[j][0], across[(j + 1) % pairs][1]) for j in range(pairs)])
        return diag * v + common.reshape(pairs, SUB, LANES) + sides

    def per_case(v):
        t = v[0]
        for j in range(1, pairs):
            t = t + v[j]
        t = t + swap_halves(t)
        return jnp.sum(t, axis=1, keepdims=True)

    def solve(residual):
        direction = residual
        gained = jnp.zeros_like(residual)
        norm_now = per_case(residual * residual)
        for iteration in range(ITERS):
            image = mass * direction + quarter_k(direction)
            step_length = (norm_now / per_case(direction * image))[None]
            gained = gained + step_length * direction
            residual = residual - step_length * image
            if iteration < ITERS - 1:
                norm_next = per_case(residual * residual)
                direction = residual + (norm_next / norm_now)[None] * direction
                norm_now = norm_next
        return gained, residual

    start0 = force0 - 4.0 * quarter_k(u0)
    start1 = force1 - 4.0 * quarter_k(u1)
    gain0, left0 = solve(start0)
    gain1, _ = solve(start1 - 5.0 * (start0 - left0) + 4.0 * mass * gain0)

    for j in range(pairs):
        back_send[2 * j] = jnp.where(low, gain0[j], swap_halves(gain1[j]))
        back_send[2 * j + 1] = jnp.where(low, swap_halves(gain0[j]), gain1[j])
    for k in range(1, count):
        there, place = other(k)
        pltpu.make_async_remote_copy(
            src_ref=back_send.at[there // spans],
            dst_ref=back_recv.at[me],
            send_sem=bsend_sem,
            recv_sem=brecv_sem,
            device_id=place,
            device_id_type=MESH,
        ).start()
    back_recv[me] = back_send[blk]
    pltpu.make_async_copy(kfull.at[rest], kfull.at[rest], ksend_sem).wait()
    pltpu.make_async_copy(send.at[others], send.at[others], send_sem).wait()
    pltpu.make_async_copy(back_recv.at[others], back_recv.at[others], brecv_sem).wait()

    first, second = [], []
    for j in range(count // 2):
        a, b = back_recv[2 * j], back_recv[2 * j + 1]
        first.append(jnp.where(low, a, swap_halves(b)))
        second.append(jnp.where(low, swap_halves(a), b))
    turned[0] = jnp.concatenate(first, 0).T
    turned[1] = jnp.concatenate(second, 0).T
    here = pl.ds(pl.multiple_of(span * rows, rows), rows)
    g0, g1 = turned[0, here, :], turned[1, here, :]
    acc1 = acc + g0
    acc2 = acc1 + g1
    vel1 = vel + acc + 0.5 * g0
    disp1 = ahead + 0.25 * g0
    disp_out[0] = disp1 + vel1 + 0.25 * acc1 + 0.25 * acc2
    vel_out[0] = vel1 + 0.5 * (acc1 + acc2)
    acc_out[0] = acc2
    pltpu.make_async_copy(back_recv.at[others], back_recv.at[others], bsend_sem).wait()


def wheel_shards(
    blks,
    spans,
    stiffness,
    mistune_table,
    sector_class,
    lumped_mass,
    near_faces,
    far_faces,
    contact_state,
    displacement,
    velocity,
    acceleration,
    load_steps,
):
    width = stiffness.shape[1]
    count = blks * spans
    vmem = pl.BlockSpec(memory_space=pltpu.VMEM)
    dma = pltpu.SemaphoreType.DMA
    return pl.pallas_call(
        functools.partial(wheel_kernel, blks, spans),
        out_shape=[jax.ShapeDtypeStruct(displacement.shape, f32)] * 3,
        in_specs=[pl.BlockSpec(memory_space=pltpu.SMEM)] + [vmem] * 10,
        out_specs=[vmem] * 3,
        scratch_shapes=[
            pltpu.VMEM((count, SUB, LANES), f32),
            pltpu.VMEM((count, SUB, LANES), f32),
            pltpu.VMEM((width, width), f32),
            pltpu.VMEM((blks, SUB, LANES), f32),
            pltpu.VMEM((count, SUB, LANES), f32),
            pltpu.VMEM((blks, width, LANES), bf16),
            pltpu.VMEM((blks, width, LANES), bf16),
            pltpu.VMEM((blks // 2, 2 * width, 4 * width), bf16),
            pltpu.VMEM((width, 2 * width), bf16),
            pltpu.VMEM((blks // 2, SUB, LANES), f32),
            pltpu.VMEM((blks // 2, SUB, LANES), f32),
            pltpu.VMEM((2, LANES, LANES), f32),
            dma,
            dma,
            dma,
            dma,
            dma,
            dma,
        ],
        compiler_params=pltpu.CompilerParams(
            collective_id=0, has_side_effects=True, vmem_limit_bytes=24 * 1024 * 1024
        ),
    )(
        sector_class,
        stiffness,
        mistune_table,
        lumped_mass,
        near_faces,
        far_faces,
        contact_state,
        displacement,
        velocity,
        acceleration,
        load_steps,
    )


def one_tile(mesh, stiffness, near_faces, displacement, load_steps):
    blks, spans = mesh.shape["blk"], mesh.shape["span"]
    sectors, width, cases = displacement.shape
    return (
        sectors == blks
        and blks % 2 == 0
        and width == LANES
        and cases == LANES
        and cases == CASES * blks * spans
        and 4 * (width // spans) == LANES
        and spans == 4
        and 4 * near_faces.shape[1] == LANES
        and load_steps.shape[0] == STEPS == 2
    )


def solution(mesh):
    placed = (
        P("span", None),
        P(None, "span"),
        P("blk"),
        P("blk", "span"),
        P("blk", None),
        P("blk", None),
        P("blk", None),
        P("blk", "span", None),
        P("blk", "span", None),
        P("blk", "span", None),
        P(None, "blk", "span", None),
    )

    def run(*arrays):
        if one_tile(mesh, arrays[0], arrays[4], arrays[7], arrays[10]):
            body = functools.partial(wheel_shards, mesh.shape["blk"], mesh.shape["span"])
        else:
            body = shards
        return jax.shard_map(
            body,
            mesh=mesh,
            in_specs=placed,
            out_specs=(P("blk", "span", None), P("blk", "span", None), P("blk", "span", None)),
            check_vma=False,
        )(*arrays)

    return run
```

```python
import functools

import jax
import jax.numpy as jnp
from jax import lax
from jax.experimental import pallas as pl
from jax.experimental.pallas import tpu as pltpu
from jax.sharding import PartitionSpec as P

BND = 64
STEPS = 2
ITERS = 5


highest = lax.Precision.HIGHEST
stick_rate = 20.0
slip_rate = 0.5
cycle_rate = 4.0

MESH = pl.DeviceIdType.MESH
LANES = 128
SUB = 8
CASES = 4
f32, bf16 = jnp.float32, jnp.bfloat16


def passed_along(block, axis, distance):
    devices = range(lax.axis_size(axis))
    route = [((i - distance) % len(devices), i) for i in devices]
    return lax.ppermute(block, axis, route)


def column_norm(vector):
    return lax.psum(jnp.sum(vector * vector, axis=(0, 1)), ("blk", "span"))


def shards(
    stiffness,
    mistune_table,
    sector_class,
    lumped_mass,
    near_faces,
    far_faces,
    contact_state,
    displacement,
    velocity,
    acceleration,
    load_steps,
):
    sectors_here, rows_here, columns = displacement.shape
    sector_width = stiffness.shape[1]
    offset = lax.axis_index("span") * rows_here
    prior_face, prior_state = passed_along((far_faces[-1], contact_state[-1]), "blk", 1)
    contact_rates = jnp.where(contact_state == 1, stick_rate, slip_rate).astype(jnp.float32)
    prior_rate = jnp.where(prior_state == 1, stick_rate, slip_rate).astype(jnp.float32)
    rate_in = jnp.concatenate([prior_rate[None], contact_rates[:-1]], 0)
    face_in = jnp.concatenate([prior_face[None], far_faces[:-1]], 0)
    left_index = jnp.arange(BND, dtype=jnp.int32)[None]
    right_index = left_index + (sector_width - BND)
    index_list = jnp.concatenate([left_index, right_index, near_faces, face_in], 1)
    face_count = near_faces.shape[1]
    row_ids = jnp.arange(rows_here, dtype=jnp.int32)
    placement_map = (index_list[:, :, None] - offset == row_ids[None, None, :]).astype(jnp.float32)
    class_ids = jnp.arange(mistune_table.shape[0], dtype=jnp.int32)
    class_map = (sector_class[:, None] == class_ids[None, :]).astype(jnp.float32)
    extra_diag = jnp.dot(class_map, mistune_table, precision=highest)
    mass_cols = lumped_mass[:, :, None]
    pick_rows = jax.vmap(lambda values, rows: values[rows])

    def stiff_op(vector):
        gathered = lax.all_gather(vector, "span", axis=1, tiled=True)
        product = jnp.einsum("rk,skc->src", stiffness, gathered, precision=highest)
        picked = pick_rows(gathered, index_list)
        left_values = picked[:, :BND]
        right_values = picked[:, BND : 2 * BND]
        near_values = picked[:, 2 * BND : 2 * BND + face_count]
        far_values = picked[:, 2 * BND + face_count :]
        prior_right, prior_near = passed_along((right_values[-1], near_values[-1]), "blk", 1)
        next_left, next_far = passed_along((left_values[0], far_values[0]), "blk", -1)
        after_left = jnp.concatenate([left_values[1:], next_left[None]], 0)
        before_right = jnp.concatenate([prior_right[None], right_values[:-1]], 0)
        after_far = jnp.concatenate([far_values[1:], next_far[None]], 0)
        before_near = jnp.concatenate([prior_near[None], near_values[:-1]], 0)
        force_left = cycle_rate * (left_values - before_right)
        force_right = cycle_rate * (right_values - after_left)
        force_out = contact_rates[:, :, None] * (near_values - after_far)
        force_in = -rate_in[:, :, None] * (before_near - far_values)
        weights = jnp.concatenate([force_left, force_right, force_out, force_in], 1)
        spread = jnp.einsum("sir,sic->src", placement_map, weights, precision=highest)
        return product + extra_diag[:, :, None] * vector + spread

    for newmark_step in range(STEPS):
        predicted = displacement + velocity + 0.25 * acceleration
        residual = (
            load_steps[newmark_step]
            - mass_cols * acceleration
            - stiff_op(predicted + 0.25 * acceleration)
        )
        solution = acceleration
        direction = residual
        norm_now = column_norm(residual)
        for iteration in range(ITERS):
            image = mass_cols * direction + 0.25 * stiff_op(direction)
            curve = lax.psum(jnp.sum(direction * image, axis=(0, 1)), ("blk", "span"))
            step_length = norm_now / curve
            solution = solution + step_length * direction
            residual = residual - step_length * image
            norm_next = column_norm(residual)
            direction = residual + norm_next / norm_now * direction
            norm_now = norm_next
        displacement = predicted + 0.25 * solution
        velocity = velocity + 0.5 * (acceleration + solution)
        acceleration = solution
    return (displacement, velocity, acceleration)


def lanes_dot(a, b):
    return lax.dot_general(a, b, (((1,), (1,)), ((), ())), preferred_element_type=f32)


def two_parts(x):
    high = x.astype(bf16).astype(f32)
    return high, x - high


def swap_halves(tile):
    return pltpu.roll(tile, CASES, 0)


def wheel_kernel(
    blks,
    spans,
    cls_hbm,
    kst_hbm,
    tab_hbm,
    mass_hbm,
    near_hbm,
    far_hbm,
    state_hbm,
    disp_hbm,
    vel_hbm,
    acc_hbm,
    load_hbm,
    disp_out,
    vel_out,
    acc_out,
    send,
    recv,
    kfull,
    back_send,
    back_recv,
    onehot_near,
    onehot_far,
    weights,
    kweights,
    mass_s,
    diag_s,
    turned,
    cls_ref,
    kst_ref,
    tab_ref,
    mass_ref,
    near_ref,
    far_ref,
    state_ref,
    disp_ref,
    vel_ref,
    acc_ref,
    load_ref,
    in_sem,
    send_sem,
    recv_sem,
    ksend_sem,
    krecv_sem,
    bsend_sem,
    brecv_sem,
):
    count = blks * spans
    blk, span = lax.axis_index("blk"), lax.axis_index("span")
    me = blk * spans + span
    rows = kst_ref.shape[0]
    width = kst_ref.shape[1]

    moves = [
        pltpu.make_async_copy(source, target, in_sem.at[i])
        for i, (source, target) in enumerate(
            (
                (disp_hbm, disp_ref),
                (vel_hbm, vel_ref),
                (acc_hbm, acc_ref),
                (load_hbm, load_ref),
                (mass_hbm, mass_ref),
                (cls_hbm, cls_ref),
                (tab_hbm, tab_ref),
                (near_hbm, near_ref),
                (far_hbm, far_ref),
                (state_hbm, state_ref),
                (kst_hbm, kst_ref),
            )
        )
    ]
    for move in moves:
        move.start()

    def other(k):
        there = lax.rem(me + k, count)
        return there, (there // spans, lax.rem(there, spans))

    barrier = pltpu.get_barrier_semaphore()
    for k in range(1, count):
        pl.semaphore_signal(barrier, inc=1, device_id=other(k)[1], device_id_type=MESH)

    for move in moves:
        move.wait()

    row = lax.broadcasted_iota(jnp.int32, (SUB, LANES), 0)
    lane = lax.broadcasted_iota(jnp.int32, (SUB, LANES), 1)
    mine = (lane // rows) == span
    low = row < CASES

    class_row = lax.broadcasted_iota(jnp.int32, tab_ref.shape, 0)
    extra = jnp.sum(jnp.where(class_row == cls_ref[0], tab_ref[...], 0.0), axis=0, keepdims=True)
    mass_here = mass_ref[...]
    rate = jnp.where(state_ref[...] == 1, 0.25 * stick_rate, 0.25 * slip_rate).astype(f32)
    contact = jnp.concatenate([near_ref[...].astype(f32), far_ref[...].astype(f32), rate, rate], 1)
    wide_mass = jnp.where(mine, jnp.concatenate([mass_here] * spans, 1), 0.0)
    wide_extra = jnp.where(mine, jnp.concatenate([0.25 * extra] * spans, 1), 0.0)
    constants = jnp.where(
        row == CASES, wide_mass, jnp.where(row == CASES + 1, wide_extra, jnp.broadcast_to(contact, (SUB, LANES)))
    )

    disp, vel, acc = disp_ref[0], vel_ref[0], acc_ref[0]
    mass_col = jnp.sum(
        jnp.where(
            lax.broadcasted_iota(jnp.int32, (rows, rows), 0) == lax.broadcasted_iota(jnp.int32, (rows, rows), 1),
            jnp.broadcast_to(mass_here, (rows, rows)),
            0.0,
        ),
        axis=1,
        keepdims=True,
    )
    inertia = mass_col * acc
    ahead = disp + vel + 0.5 * acc
    later = ahead + vel + 1.5 * acc
    stacked = jnp.concatenate([ahead, load_ref[0, 0] - inertia, later, load_ref[1, 0] - inertia], 0)
    flipped = stacked.T
    for j in range(count // 2):
        tile = flipped[SUB * j : SUB * (j + 1)]
        send[2 * j] = jnp.where(low, tile, constants)
        send[2 * j + 1] = jnp.where(low, swap_halves(tile), constants)

    pl.semaphore_wait(barrier, count - 1)
    for k in range(1, spans):
        pltpu.make_async_remote_copy(
            src_ref=kst_ref,
            dst_ref=kfull.at[pl.ds(pl.multiple_of(span * rows, rows), rows)],
            send_sem=ksend_sem,
            recv_sem=krecv_sem,
            device_id=(blk, lax.rem(span + k, spans)),
            device_id_type=MESH,
        ).start()
    for k in range(1, count):
        there, place = other(k)
        pltpu.make_async_remote_copy(
            src_ref=send.at[there],
            dst_ref=recv.at[me],
            send_sem=send_sem,
            recv_sem=recv_sem,
            device_id=place,
            device_id_type=MESH,
        ).start()
    recv[me] = send[me]
    kfull[pl.ds(pl.multiple_of(span * rows, rows), rows), :] = kst_ref[...]

    rest = pl.ds(0, (spans - 1) * rows)
    pltpu.make_async_copy(kfull.at[rest], kfull.at[rest], krecv_sem).wait()
    kscaled = 0.25 * kfull[...]
    khigh, klow = two_parts(kscaled)
    kweights[:, :width] = khigh.astype(bf16)
    kweights[:, width:] = klow.astype(bf16)

    others = pl.ds(0, count - 1)
    pltpu.make_async_copy(recv.at[others], recv.at[others], recv_sem).wait()

    sub_index = lax.broadcasted_iota(jnp.int32, (width, LANES), 0).astype(f32)
    face_lane = lax.broadcasted_iota(jnp.int32, (1, LANES), 1) < near_ref.shape[1]
    ones = jnp.ones((2 * SUB, LANES), bf16)
    near_diag, far_diag, own = [], [], []
    for b in range(blks):
        tiles = [recv[b * spans + s] for s in range(spans)]
        total = tiles[0]
        for tile in tiles[1:]:
            total = total + tile
        own.append((total[CASES : CASES + 1], total[CASES + 1 : CASES + 2]))
        faces = tiles[0][CASES + 2 : CASES + 3]
        near_row = faces
        far_row = pltpu.roll(faces, LANES - near_ref.shape[1], 1)
        rate_row = jnp.where(face_lane, pltpu.roll(faces, LANES - 2 * near_ref.shape[1], 1), 0.0)
        near_hot = jnp.where(sub_index == near_row, rate_row, 0.0).astype(bf16)
        far_hot = jnp.where((sub_index == far_row) & face_lane, 1.0, 0.0).astype(bf16)
        onehot_near[b] = near_hot
        onehot_far[b] = far_hot
        near_diag.append(lanes_dot(ones, near_hot))
        far_diag.append(lanes_dot(jnp.broadcast_to(rate_row, (2 * SUB, LANES)).astype(bf16), far_hot))

    n_row = lax.broadcasted_iota(jnp.int32, (width, width), 0)
    n_col = lax.broadcasted_iota(jnp.int32, (width, width), 1)
    tie = 0.25 * cycle_rate
    shift_down = jnp.where((n_row == n_col + (width - BND)) & (n_col < BND), tie, 0.0)
    shift_up = jnp.where((n_col == n_row + (width - BND)) & (n_row < BND), tie, 0.0)
    lane_row = lax.broadcasted_iota(jnp.int32, (1, LANES), 1)
    ends = jnp.where(lane_row < BND, tie, 0.0) + jnp.where(lane_row >= width - BND, tie, 0.0)
    for b in range(blks):
        prev = (b - 1) % blks
        j, half = divmod(b, 2)
        mass_s[j, CASES * half : CASES * (half + 1), :] = jnp.broadcast_to(own[b][0], (CASES, LANES))
        diag_row = own[b][1] + ends + near_diag[b][0:1] + far_diag[prev][0:1]
        diag_s[j, CASES * half : CASES * (half + 1), :] = jnp.broadcast_to(diag_row, (CASES, LANES))
        before = -(lanes_dot(onehot_near[prev], onehot_far[prev]) + shift_down)
        after = -(lanes_dot(onehot_far[b], onehot_near[b]) + shift_up)
        group = j if half == 0 else (j + 1) % (blks // 2)
        base = 2 * width * half
        for part, block in enumerate((before, after)):
            high, small = two_parts(block)
            weights[group, width * part : width * (part + 1), base : base + width] = high.astype(bf16)
            weights[group, width * part : width * (part + 1), base + width : base + 2 * width] = small.astype(bf16)

    pairs = blks // 2
    group_of = lane // rows
    pieces = [[] for _ in range(4)]
    for j in range(pairs):
        parts = [
            jnp.where(low, recv[2 * j * spans + s], swap_halves(recv[(2 * j + 1) * spans + s])) for s in range(spans)
        ]
        for k in range(4):
            value = None
            for s in range(spans):
                turn = (rows * (s - k)) % LANES
                moved = pltpu.roll(parts[s], turn, 1) if turn else parts[s]
                value = moved if value is None else jnp.where(group_of == s, moved, value)
            pieces[k].append(value)
    u0, force0, u1, force1 = (jnp.stack(p) for p in pieces)
    mass = mass_s[...]
    diag = diag_s[...]

    def quarter_k(v):
        high, small = two_parts(v)
        both = jnp.concatenate([high.reshape(pairs * SUB, LANES), small.reshape(pairs * SUB, LANES)], 0).astype(bf16)
        p = jnp.dot(both, kweights[...], preferred_element_type=f32)
        h = pairs * SUB
        common = p[:h, :width] + (p[h:, :width] + p[:h, width:])
        tiles = []
        for j in range(pairs):
            t = jnp.concatenate([swap_halves(high[j]), swap_halves(small[j])], 0)
            tiles.append(t.astype(bf16))
        across = []
        for j in range(pairs):
            lhs = jnp.concatenate([tiles[j - 1], tiles[j]], 1)
            g = jnp.dot(lhs, weights[j], preferred_element_type=f32)
            even = g[:SUB, :width] + (g[SUB:, :width] + g[:SUB, width : 2 * width])
            odd = g[:SUB, 2 * width : 3 * width] + (g[SUB:, 2 * width : 3 * width] + g[:SUB, 3 * width :])
            across.append((even, odd))
        sides = jnp.stack([jnp.where(low, across[j][0], across[(j + 1) % pairs][1]) for j in range(pairs)])
        return diag * v + common.reshape(pairs, SUB, LANES) + sides

    def per_case(v):
        t = v[0]
        for j in range(1, pairs):
            t = t + v[j]
        t = t + swap_halves(t)
        return jnp.sum(t, axis=1, keepdims=True)

    def solve(residual):
        direction = residual
        gained = jnp.zeros_like(residual)
        norm_now = per_case(residual * residual)
        for iteration in range(ITERS):
            image = mass * direction + quarter_k(direction)
            step_length = (norm_now / per_case(direction * image))[None]
            gained = gained + step_length * direction
            residual = residual - step_length * image
            if iteration < ITERS - 1:
                norm_next = per_case(residual * residual)
                direction = residual + (norm_next / norm_now)[None] * direction
                norm_now = norm_next
        return gained, residual

    start0 = force0 - 4.0 * quarter_k(u0)
    start1 = force1 - 4.0 * quarter_k(u1)
    gain0, left0 = solve(start0)
    gain1, _ = solve(start1 - 5.0 * (start0 - left0) + 4.0 * mass * gain0)

    for j in range(pairs):
        back_send[2 * j] = jnp.where(low, gain0[j], swap_halves(gain1[j]))
        back_send[2 * j + 1] = jnp.where(low, swap_halves(gain0[j]), gain1[j])
    for k in range(1, count):
        there, place = other(k)
        pltpu.make_async_remote_copy(
            src_ref=back_send.at[there // spans],
            dst_ref=back_recv.at[me],
            send_sem=bsend_sem,
            recv_sem=brecv_sem,
            device_id=place,
            device_id_type=MESH,
        ).start()
    back_recv[me] = back_send[blk]
    pltpu.make_async_copy(kfull.at[rest], kfull.at[rest], ksend_sem).wait()
    pltpu.make_async_copy(send.at[others], send.at[others], send_sem).wait()
    pltpu.make_async_copy(back_recv.at[others], back_recv.at[others], brecv_sem).wait()

    first, second = [], []
    for j in range(count // 2):
        a, b = back_recv[2 * j], back_recv[2 * j + 1]
        first.append(jnp.where(low, a, swap_halves(b)))
        second.append(jnp.where(low, swap_halves(a), b))
    turned[0] = jnp.concatenate(first, 0).T
    turned[1] = jnp.concatenate(second, 0).T
    here = pl.ds(pl.multiple_of(span * rows, rows), rows)
    g0, g1 = turned[0, here, :], turned[1, here, :]
    acc1 = acc + g0
    acc2 = acc1 + g1
    vel1 = vel + acc + 0.5 * g0
    disp1 = ahead + 0.25 * g0
    disp_out[0] = disp1 + vel1 + 0.25 * acc1 + 0.25 * acc2
    vel_out[0] = vel1 + 0.5 * (acc1 + acc2)
    acc_out[0] = acc2
    pltpu.make_async_copy(back_recv.at[others], back_recv.at[others], bsend_sem).wait()


def hand_over(a_in, b_in, c_in, a_out, b_out, c_out, sem):
    moves = [
        pltpu.make_async_copy(source, target, sem.at[i])
        for i, (source, target) in enumerate(((a_in, a_out), (b_in, b_out), (c_in, c_out)))
    ]
    for move in moves:
        move.start()
    for move in moves:
        move.wait()


def wheel_shards(
    blks,
    spans,
    stiffness,
    mistune_table,
    sector_class,
    lumped_mass,
    near_faces,
    far_faces,
    contact_state,
    displacement,
    velocity,
    acceleration,
    load_steps,
):
    width = stiffness.shape[1]
    count = blks * spans
    operands = (
        sector_class,
        stiffness,
        mistune_table,
        lumped_mass,
        near_faces,
        far_faces,
        contact_state,
        displacement,
        velocity,
        acceleration,
        load_steps,
    )
    vmem = pl.BlockSpec(memory_space=pltpu.VMEM)
    dma = pltpu.SemaphoreType.DMA
    results = pl.pallas_call(
        functools.partial(wheel_kernel, blks, spans),
        out_shape=[jax.ShapeDtypeStruct(displacement.shape, f32)] * 3,
        in_specs=[pl.BlockSpec(memory_space=pltpu.HBM)] * 11,
        out_specs=[vmem] * 3,
        scratch_shapes=[
            pltpu.VMEM((count, SUB, LANES), f32),
            pltpu.VMEM((count, SUB, LANES), f32),
            pltpu.VMEM((width, width), f32),
            pltpu.VMEM((blks, SUB, LANES), f32),
            pltpu.VMEM((count, SUB, LANES), f32),
            pltpu.VMEM((blks, width, LANES), bf16),
            pltpu.VMEM((blks, width, LANES), bf16),
            pltpu.VMEM((blks // 2, 2 * width, 4 * width), bf16),
            pltpu.VMEM((width, 2 * width), bf16),
            pltpu.VMEM((blks // 2, SUB, LANES), f32),
            pltpu.VMEM((blks // 2, SUB, LANES), f32),
            pltpu.VMEM((2, LANES, LANES), f32),
            pltpu.SMEM(sector_class.shape, jnp.int32),
            *(pltpu.VMEM(a.shape, a.dtype) for a in operands[1:]),
            pltpu.SemaphoreType.DMA((len(operands),)),
            dma,
            dma,
            dma,
            dma,
            dma,
            dma,
        ],
        compiler_params=pltpu.CompilerParams(
            collective_id=0, has_side_effects=True
        ),
    )(*operands)
    return pl.pallas_call(
        hand_over,
        out_shape=[jax.ShapeDtypeStruct(displacement.shape, f32)] * 3,
        in_specs=[pl.BlockSpec(memory_space=pl.ANY)] * 3,
        out_specs=[pl.BlockSpec(memory_space=pltpu.HBM)] * 3,
        scratch_shapes=[pltpu.SemaphoreType.DMA((3,))],
    )(*results)


def one_tile(mesh, stiffness, near_faces, displacement, load_steps):
    blks, spans = mesh.shape["blk"], mesh.shape["span"]
    sectors, width, cases = displacement.shape
    return (
        sectors == blks
        and blks % 2 == 0
        and width == LANES
        and cases == LANES
        and cases == CASES * blks * spans
        and 4 * (width // spans) == LANES
        and spans == 4
        and 4 * near_faces.shape[1] == LANES
        and load_steps.shape[0] == STEPS == 2
    )


def solution(mesh):
    placed = (
        P("span", None),
        P(None, "span"),
        P("blk"),
        P("blk", "span"),
        P("blk", None),
        P("blk", None),
        P("blk", None),
        P("blk", "span", None),
        P("blk", "span", None),
        P("blk", "span", None),
        P(None, "blk", "span", None),
    )

    def run(*arrays):
        if one_tile(mesh, arrays[0], arrays[4], arrays[7], arrays[10]):
            body = functools.partial(wheel_shards, mesh.shape["blk"], mesh.shape["span"])
        else:
            body = shards
        return jax.shard_map(
            body,
            mesh=mesh,
            in_specs=placed,
            out_specs=(P("blk", "span", None), P("blk", "span", None), P("blk", "span", None)),
            check_vma=False,
        )(*arrays)

    return run
```

```python
import functools

import jax
import jax.numpy as jnp
from jax import lax
from jax.experimental import pallas as pl
from jax.experimental.pallas import tpu as pltpu
from jax.sharding import PartitionSpec as P

BND = 64
STEPS = 2
ITERS = 5


highest = lax.Precision.HIGHEST
stick_rate = 20.0
slip_rate = 0.5
cycle_rate = 4.0

MESH = pl.DeviceIdType.MESH
LANES = 128
SUB = 8
CASES = 4
f32, bf16 = jnp.float32, jnp.bfloat16


def passed_along(block, axis, distance):
    devices = range(lax.axis_size(axis))
    route = [((i - distance) % len(devices), i) for i in devices]
    return lax.ppermute(block, axis, route)


def column_norm(vector):
    return lax.psum(jnp.sum(vector * vector, axis=(0, 1)), ("blk", "span"))


def shards(
    stiffness,
    mistune_table,
    sector_class,
    lumped_mass,
    near_faces,
    far_faces,
    contact_state,
    displacement,
    velocity,
    acceleration,
    load_steps,
):
    sectors_here, rows_here, columns = displacement.shape
    sector_width = stiffness.shape[1]
    offset = lax.axis_index("span") * rows_here
    prior_face, prior_state = passed_along((far_faces[-1], contact_state[-1]), "blk", 1)
    contact_rates = jnp.where(contact_state == 1, stick_rate, slip_rate).astype(jnp.float32)
    prior_rate = jnp.where(prior_state == 1, stick_rate, slip_rate).astype(jnp.float32)
    rate_in = jnp.concatenate([prior_rate[None], contact_rates[:-1]], 0)
    face_in = jnp.concatenate([prior_face[None], far_faces[:-1]], 0)
    left_index = jnp.arange(BND, dtype=jnp.int32)[None]
    right_index = left_index + (sector_width - BND)
    index_list = jnp.concatenate([left_index, right_index, near_faces, face_in], 1)
    face_count = near_faces.shape[1]
    row_ids = jnp.arange(rows_here, dtype=jnp.int32)
    placement_map = (index_list[:, :, None] - offset == row_ids[None, None, :]).astype(jnp.float32)
    class_ids = jnp.arange(mistune_table.shape[0], dtype=jnp.int32)
    class_map = (sector_class[:, None] == class_ids[None, :]).astype(jnp.float32)
    extra_diag = jnp.dot(class_map, mistune_table, precision=highest)
    mass_cols = lumped_mass[:, :, None]
    pick_rows = jax.vmap(lambda values, rows: values[rows])

    def stiff_op(vector):
        gathered = lax.all_gather(vector, "span", axis=1, tiled=True)
        product = jnp.einsum("rk,skc->src", stiffness, gathered, precision=highest)
        picked = pick_rows(gathered, index_list)
        left_values = picked[:, :BND]
        right_values = picked[:, BND : 2 * BND]
        near_values = picked[:, 2 * BND : 2 * BND + face_count]
        far_values = picked[:, 2 * BND + face_count :]
        prior_right, prior_near = passed_along((right_values[-1], near_values[-1]), "blk", 1)
        next_left, next_far = passed_along((left_values[0], far_values[0]), "blk", -1)
        after_left = jnp.concatenate([left_values[1:], next_left[None]], 0)
        before_right = jnp.concatenate([prior_right[None], right_values[:-1]], 0)
        after_far = jnp.concatenate([far_values[1:], next_far[None]], 0)
        before_near = jnp.concatenate([prior_near[None], near_values[:-1]], 0)
        force_left = cycle_rate * (left_values - before_right)
        force_right = cycle_rate * (right_values - after_left)
        force_out = contact_rates[:, :, None] * (near_values - after_far)
        force_in = -rate_in[:, :, None] * (before_near - far_values)
        weights = jnp.concatenate([force_left, force_right, force_out, force_in], 1)
        spread = jnp.einsum("sir,sic->src", placement_map, weights, precision=highest)
        return product + extra_diag[:, :, None] * vector + spread

    for newmark_step in range(STEPS):
        predicted = displacement + velocity + 0.25 * acceleration
        residual = (
            load_steps[newmark_step]
            - mass_cols * acceleration
            - stiff_op(predicted + 0.25 * acceleration)
        )
        solution = acceleration
        direction = residual
        norm_now = column_norm(residual)
        for iteration in range(ITERS):
            image = mass_cols * direction + 0.25 * stiff_op(direction)
            curve = lax.psum(jnp.sum(direction * image, axis=(0, 1)), ("blk", "span"))
            step_length = norm_now / curve
            solution = solution + step_length * direction
            residual = residual - step_length * image
            norm_next = column_norm(residual)
            direction = residual + norm_next / norm_now * direction
            norm_now = norm_next
        displacement = predicted + 0.25 * solution
        velocity = velocity + 0.5 * (acceleration + solution)
        acceleration = solution
    return (displacement, velocity, acceleration)


def lanes_dot(a, b):
    return lax.dot_general(a, b, (((1,), (1,)), ((), ())), preferred_element_type=f32)


def two_parts(x):
    high = x.astype(bf16).astype(f32)
    return high, x - high


def swap_halves(tile):
    return pltpu.roll(tile, CASES, 0)


def wheel_kernel(
    blks,
    spans,
    cls_hbm,
    kst_hbm,
    tab_hbm,
    mass_hbm,
    near_hbm,
    far_hbm,
    state_hbm,
    disp_hbm,
    vel_hbm,
    acc_hbm,
    load_hbm,
    first_out,
    second_out,
    send,
    recv,
    kfull,
    back_send,
    back_recv,
    onehot_near,
    onehot_far,
    weights,
    kweights,
    mass_s,
    diag_s,
    turned,
    cls_ref,
    kst_ref,
    tab_ref,
    mass_ref,
    near_ref,
    far_ref,
    state_ref,
    disp_ref,
    vel_ref,
    acc_ref,
    load_ref,
    in_sem,
    send_sem,
    recv_sem,
    ksend_sem,
    krecv_sem,
    bsend_sem,
    brecv_sem,
):
    count = blks * spans
    blk, span = lax.axis_index("blk"), lax.axis_index("span")
    me = blk * spans + span
    rows = kst_ref.shape[0]
    width = kst_ref.shape[1]

    moves = [
        pltpu.make_async_copy(source, target, in_sem.at[i])
        for i, (source, target) in enumerate(
            (
                (disp_hbm, disp_ref),
                (vel_hbm, vel_ref),
                (acc_hbm, acc_ref),
                (load_hbm, load_ref),
                (mass_hbm, mass_ref),
                (cls_hbm, cls_ref),
                (tab_hbm, tab_ref),
                (near_hbm, near_ref),
                (far_hbm, far_ref),
                (state_hbm, state_ref),
                (kst_hbm, kst_ref),
            )
        )
    ]
    for move in moves:
        move.start()

    def other(k):
        there = lax.rem(me + k, count)
        return there, (there // spans, lax.rem(there, spans))

    barrier = pltpu.get_barrier_semaphore()
    for k in range(1, count):
        pl.semaphore_signal(barrier, inc=1, device_id=other(k)[1], device_id_type=MESH)

    for move in moves:
        move.wait()

    row = lax.broadcasted_iota(jnp.int32, (SUB, LANES), 0)
    lane = lax.broadcasted_iota(jnp.int32, (SUB, LANES), 1)
    mine = (lane // rows) == span
    low = row < CASES

    class_row = lax.broadcasted_iota(jnp.int32, tab_ref.shape, 0)
    extra = jnp.sum(jnp.where(class_row == cls_ref[0], tab_ref[...], 0.0), axis=0, keepdims=True)
    mass_here = mass_ref[...]
    rate = jnp.where(state_ref[...] == 1, 0.25 * stick_rate, 0.25 * slip_rate).astype(f32)
    contact = jnp.concatenate([near_ref[...].astype(f32), far_ref[...].astype(f32), rate, rate], 1)
    wide_mass = jnp.where(mine, jnp.concatenate([mass_here] * spans, 1), 0.0)
    wide_extra = jnp.where(mine, jnp.concatenate([0.25 * extra] * spans, 1), 0.0)
    constants = jnp.where(
        row == CASES, wide_mass, jnp.where(row == CASES + 1, wide_extra, jnp.broadcast_to(contact, (SUB, LANES)))
    )

    disp, vel, acc = disp_ref[0], vel_ref[0], acc_ref[0]
    mass_col = jnp.sum(
        jnp.where(
            lax.broadcasted_iota(jnp.int32, (rows, rows), 0) == lax.broadcasted_iota(jnp.int32, (rows, rows), 1),
            jnp.broadcast_to(mass_here, (rows, rows)),
            0.0,
        ),
        axis=1,
        keepdims=True,
    )
    inertia = mass_col * acc
    ahead = disp + vel + 0.5 * acc
    later = ahead + vel + 1.5 * acc
    stacked = jnp.concatenate([ahead, load_ref[0, 0] - inertia, later, load_ref[1, 0] - inertia], 0)
    flipped = stacked.T
    for j in range(count // 2):
        tile = flipped[SUB * j : SUB * (j + 1)]
        send[2 * j] = jnp.where(low, tile, constants)
        send[2 * j + 1] = jnp.where(low, swap_halves(tile), constants)

    pl.semaphore_wait(barrier, count - 1)
    for k in range(1, spans):
        pltpu.make_async_remote_copy(
            src_ref=kst_ref,
            dst_ref=kfull.at[pl.ds(pl.multiple_of(span * rows, rows), rows)],
            send_sem=ksend_sem,
            recv_sem=krecv_sem,
            device_id=(blk, lax.rem(span + k, spans)),
            device_id_type=MESH,
        ).start()
    for k in range(1, count):
        there, place = other(k)
        pltpu.make_async_remote_copy(
            src_ref=send.at[there],
            dst_ref=recv.at[me],
            send_sem=send_sem,
            recv_sem=recv_sem,
            device_id=place,
            device_id_type=MESH,
        ).start()
    recv[me] = send[me]
    kfull[pl.ds(pl.multiple_of(span * rows, rows), rows), :] = kst_ref[...]

    rest = pl.ds(0, (spans - 1) * rows)
    pltpu.make_async_copy(kfull.at[rest], kfull.at[rest], krecv_sem).wait()
    kscaled = 0.25 * kfull[...]
    khigh, klow = two_parts(kscaled)
    kweights[:, :width] = khigh.astype(bf16)
    kweights[:, width:] = klow.astype(bf16)

    others = pl.ds(0, count - 1)
    pltpu.make_async_copy(recv.at[others], recv.at[others], recv_sem).wait()

    sub_index = lax.broadcasted_iota(jnp.int32, (width, LANES), 0).astype(f32)
    face_lane = lax.broadcasted_iota(jnp.int32, (1, LANES), 1) < near_ref.shape[1]
    ones = jnp.ones((2 * SUB, LANES), bf16)
    near_diag, far_diag, own = [], [], []
    for b in range(blks):
        tiles = [recv[b * spans + s] for s in range(spans)]
        total = tiles[0]
        for tile in tiles[1:]:
            total = total + tile
        own.append((total[CASES : CASES + 1], total[CASES + 1 : CASES + 2]))
        faces = tiles[0][CASES + 2 : CASES + 3]
        near_row = faces
        far_row = pltpu.roll(faces, LANES - near_ref.shape[1], 1)
        rate_row = jnp.where(face_lane, pltpu.roll(faces, LANES - 2 * near_ref.shape[1], 1), 0.0)
        near_hot = jnp.where(sub_index == near_row, rate_row, 0.0).astype(bf16)
        far_hot = jnp.where((sub_index == far_row) & face_lane, 1.0, 0.0).astype(bf16)
        onehot_near[b] = near_hot
        onehot_far[b] = far_hot
        near_diag.append(lanes_dot(ones, near_hot))
        far_diag.append(lanes_dot(jnp.broadcast_to(rate_row, (2 * SUB, LANES)).astype(bf16), far_hot))

    n_row = lax.broadcasted_iota(jnp.int32, (width, width), 0)
    n_col = lax.broadcasted_iota(jnp.int32, (width, width), 1)
    tie = 0.25 * cycle_rate
    shift_down = jnp.where((n_row == n_col + (width - BND)) & (n_col < BND), tie, 0.0)
    shift_up = jnp.where((n_col == n_row + (width - BND)) & (n_row < BND), tie, 0.0)
    lane_row = lax.broadcasted_iota(jnp.int32, (1, LANES), 1)
    ends = jnp.where(lane_row < BND, tie, 0.0) + jnp.where(lane_row >= width - BND, tie, 0.0)
    for b in range(blks):
        prev = (b - 1) % blks
        j, half = divmod(b, 2)
        mass_s[j, CASES * half : CASES * (half + 1), :] = jnp.broadcast_to(own[b][0], (CASES, LANES))
        diag_row = own[b][1] + ends + near_diag[b][0:1] + far_diag[prev][0:1]
        diag_s[j, CASES * half : CASES * (half + 1), :] = jnp.broadcast_to(diag_row, (CASES, LANES))
        before = -(lanes_dot(onehot_near[prev], onehot_far[prev]) + shift_down)
        after = -(lanes_dot(onehot_far[b], onehot_near[b]) + shift_up)
        group = j if half == 0 else (j + 1) % (blks // 2)
        base = 2 * width * half
        for part, block in enumerate((before, after)):
            high, small = two_parts(block)
            weights[group, width * part : width * (part + 1), base : base + width] = high.astype(bf16)
            weights[group, width * part : width * (part + 1), base + width : base + 2 * width] = small.astype(bf16)

    pairs = blks // 2
    group_of = lane // rows
    pieces = [[] for _ in range(4)]
    for j in range(pairs):
        parts = [
            jnp.where(low, recv[2 * j * spans + s], swap_halves(recv[(2 * j + 1) * spans + s])) for s in range(spans)
        ]
        for k in range(4):
            value = None
            for s in range(spans):
                turn = (rows * (s - k)) % LANES
                moved = pltpu.roll(parts[s], turn, 1) if turn else parts[s]
                value = moved if value is None else jnp.where(group_of == s, moved, value)
            pieces[k].append(value)
    u0, force0, u1, force1 = (jnp.stack(p) for p in pieces)
    mass = mass_s[...]
    diag = diag_s[...]

    def quarter_k(v):
        high, small = two_parts(v)
        both = jnp.concatenate([high.reshape(pairs * SUB, LANES), small.reshape(pairs * SUB, LANES)], 0).astype(bf16)
        p = jnp.dot(both, kweights[...], preferred_element_type=f32)
        h = pairs * SUB
        common = p[:h, :width] + (p[h:, :width] + p[:h, width:])
        tiles = []
        for j in range(pairs):
            t = jnp.concatenate([swap_halves(high[j]), swap_halves(small[j])], 0)
            tiles.append(t.astype(bf16))
        across = []
        for j in range(pairs):
            lhs = jnp.concatenate([tiles[j - 1], tiles[j]], 1)
            g = jnp.dot(lhs, weights[j], preferred_element_type=f32)
            even = g[:SUB, :width] + (g[SUB:, :width] + g[:SUB, width : 2 * width])
            odd = g[:SUB, 2 * width : 3 * width] + (g[SUB:, 2 * width : 3 * width] + g[:SUB, 3 * width :])
            across.append((even, odd))
        sides = jnp.stack([jnp.where(low, across[j][0], across[(j + 1) % pairs][1]) for j in range(pairs)])
        return diag * v + common.reshape(pairs, SUB, LANES) + sides

    def per_case(v):
        t = v[0]
        for j in range(1, pairs):
            t = t + v[j]
        t = t + swap_halves(t)
        return jnp.sum(t, axis=1, keepdims=True)

    def solve(residual):
        direction = residual
        gained = jnp.zeros_like(residual)
        norm_now = per_case(residual * residual)
        for iteration in range(ITERS):
            image = mass * direction + quarter_k(direction)
            step_length = (norm_now / per_case(direction * image))[None]
            gained = gained + step_length * direction
            residual = residual - step_length * image
            if iteration < ITERS - 1:
                norm_next = per_case(residual * residual)
                direction = residual + (norm_next / norm_now)[None] * direction
                norm_now = norm_next
        return gained, residual

    start0 = force0 - 4.0 * quarter_k(u0)
    start1 = force1 - 4.0 * quarter_k(u1)
    gain0, left0 = solve(start0)
    gain1, _ = solve(start1 - 5.0 * (start0 - left0) + 4.0 * mass * gain0)

    for j in range(pairs):
        back_send[2 * j] = jnp.where(low, gain0[j], swap_halves(gain1[j]))
        back_send[2 * j + 1] = jnp.where(low, swap_halves(gain0[j]), gain1[j])
    for k in range(1, count):
        there, place = other(k)
        pltpu.make_async_remote_copy(
            src_ref=back_send.at[there // spans],
            dst_ref=back_recv.at[me],
            send_sem=bsend_sem,
            recv_sem=brecv_sem,
            device_id=place,
            device_id_type=MESH,
        ).start()
    back_recv[me] = back_send[blk]
    pltpu.make_async_copy(kfull.at[rest], kfull.at[rest], ksend_sem).wait()
    pltpu.make_async_copy(send.at[others], send.at[others], send_sem).wait()
    pltpu.make_async_copy(back_recv.at[others], back_recv.at[others], brecv_sem).wait()

    first, second = [], []
    for j in range(count // 2):
        a, b = back_recv[2 * j], back_recv[2 * j + 1]
        first.append(jnp.where(low, a, swap_halves(b)))
        second.append(jnp.where(low, swap_halves(a), b))
    turned[0] = jnp.concatenate(first, 0).T
    turned[1] = jnp.concatenate(second, 0).T
    here = pl.ds(pl.multiple_of(span * rows, rows), rows)
    first_out[0] = turned[0, here, :]
    second_out[0] = turned[1, here, :]
    pltpu.make_async_copy(back_recv.at[others], back_recv.at[others], bsend_sem).wait()


def wheel_shards(
    blks,
    spans,
    stiffness,
    mistune_table,
    sector_class,
    lumped_mass,
    near_faces,
    far_faces,
    contact_state,
    displacement,
    velocity,
    acceleration,
    load_steps,
):
    width = stiffness.shape[1]
    count = blks * spans
    operands = (
        sector_class,
        stiffness,
        mistune_table,
        lumped_mass,
        near_faces,
        far_faces,
        contact_state,
        displacement,
        velocity,
        acceleration,
        load_steps,
    )
    vmem = pl.BlockSpec(memory_space=pltpu.VMEM)
    dma = pltpu.SemaphoreType.DMA
    results = pl.pallas_call(
        functools.partial(wheel_kernel, blks, spans),
        out_shape=[jax.ShapeDtypeStruct(displacement.shape, f32)] * 2,
        in_specs=[pl.BlockSpec(memory_space=pltpu.HBM)] * 11,
        out_specs=[vmem] * 2,
        scratch_shapes=[
            pltpu.VMEM((count, SUB, LANES), f32),
            pltpu.VMEM((count, SUB, LANES), f32),
            pltpu.VMEM((width, width), f32),
            pltpu.VMEM((blks, SUB, LANES), f32),
            pltpu.VMEM((count, SUB, LANES), f32),
            pltpu.VMEM((blks, width, LANES), bf16),
            pltpu.VMEM((blks, width, LANES), bf16),
            pltpu.VMEM((blks // 2, 2 * width, 4 * width), bf16),
            pltpu.VMEM((width, 2 * width), bf16),
            pltpu.VMEM((blks // 2, SUB, LANES), f32),
            pltpu.VMEM((blks // 2, SUB, LANES), f32),
            pltpu.VMEM((2, LANES, LANES), f32),
            pltpu.SMEM(sector_class.shape, jnp.int32),
            *(pltpu.VMEM(a.shape, a.dtype) for a in operands[1:]),
            pltpu.SemaphoreType.DMA((len(operands),)),
            dma,
            dma,
            dma,
            dma,
            dma,
            dma,
        ],
        compiler_params=pltpu.CompilerParams(
            collective_id=0, has_side_effects=True
        ),
    )(*operands)
    first, second = results
    acc1 = acceleration + first
    acc2 = acc1 + second
    vel1 = velocity + acceleration + 0.5 * first
    disp1 = displacement + velocity + 0.5 * acceleration + 0.25 * first
    return (
        disp1 + vel1 + 0.25 * acc1 + 0.25 * acc2,
        vel1 + 0.5 * (acc1 + acc2),
        acc2,
    )


def one_tile(mesh, stiffness, near_faces, displacement, load_steps):
    blks, spans = mesh.shape["blk"], mesh.shape["span"]
    sectors, width, cases = displacement.shape
    return (
        sectors == blks
        and blks % 2 == 0
        and width == LANES
        and cases == LANES
        and cases == CASES * blks * spans
        and 4 * (width // spans) == LANES
        and spans == 4
        and 4 * near_faces.shape[1] == LANES
        and load_steps.shape[0] == STEPS == 2
    )


def solution(mesh):
    placed = (
        P("span", None),
        P(None, "span"),
        P("blk"),
        P("blk", "span"),
        P("blk", None),
        P("blk", None),
        P("blk", None),
        P("blk", "span", None),
        P("blk", "span", None),
        P("blk", "span", None),
        P(None, "blk", "span", None),
    )

    def run(*arrays):
        if one_tile(mesh, arrays[0], arrays[4], arrays[7], arrays[10]):
            body = functools.partial(wheel_shards, mesh.shape["blk"], mesh.shape["span"])
        else:
            body = shards
        return jax.shard_map(
            body,
            mesh=mesh,
            in_specs=placed,
            out_specs=(P("blk", "span", None), P("blk", "span", None), P("blk", "span", None)),
            check_vma=False,
        )(*arrays)

    return run
```
